32 devices in a mesh: img: 2 (over core), fsdp: 16 (over z, y, x).
Axes of the slice: x: 2, y: 2, z: 4, core: 2. Of those that a mesh axis runs over, the one named last changes fastest.
Arguments:
- text_states: bfloat16 [4096, 8192], P('fsdp')
- text_gain: float32 [8192], replicated, may hold values from 0.1 to 1.9
- vision: bfloat16 [2, 128, 8192], P('img', 'fsdp'), may hold values from -6 to 6
- q_weight: bfloat16 [8192, 1024], P('fsdp', 'img'), may hold values from -0.0625 to 0.0625
- k_weight: bfloat16 [8192, 256], P('fsdp', 'img'), may hold values from -0.0625 to 0.0625
- v_weight: bfloat16 [8192, 256], P('fsdp', 'img'), may hold values from -0.0625 to 0.0625
- q_gain: float32 [128], replicated, may hold values from 1 to 16
- k_gain: float32 [128], replicated, may hold values from 1 to 16
- owners: int32 [64, 4], P('fsdp'), may hold values from 0 to 1
- counts: int32 [64], P('fsdp'), may hold values from 0 to 4
- gate_value: float32 [1], replicated, may hold values from 0.3 to 1.5
Outputs:
- attended: bfloat16 [4096, 1024], P('fsdp', 'img')
The draws below stay inside these ranges and needn't reach their ends.
All inputs are finite; a program needn't handle non-finite values.
Results may differ from the reference program's by a relative error of at most 0.025.
The reference program's roundings to bfloat16 on the way (of `normed`, `queries`, `keys` and `weights`) count: a program that leaves them out, or rounds other values in their place, can miss the bound.
Values may be sent and summed in bfloat16 or wider, within the bound.
A program may use at most 64 MiB of HBM per device.

```python
import math
import jax
import jax.numpy as jnp
from jax import lax

D = 8192
HD = 128
QH_DEV = 4
BLK = 64
LIST = 4
TOKENS = 4096
NBLK = 64
VIS = 128
IMAGES = 2
KVH = 2
QHEADS = 8


def draw_text_states(key, part):
    key = jax.random.fold_in(key, 13)
    first, second, third = jax.random.split(key, 3)
    base = jax.random.normal(first, (TOKENS, D), jnp.float32)
    row_scale = jnp.exp(jax.random.uniform(second, (TOKENS, 1), jnp.float32, math.log(0.5), math.log(5.0)))
    column_scale = jnp.exp(jax.random.uniform(third, (1, D), jnp.float32, math.log(0.3), math.log(3.0)))
    return (base * row_scale * column_scale).astype(jnp.bfloat16)


def gain_helper(key):
    return jnp.exp(jax.random.uniform(key, (HD,), jnp.float32, 0.0, math.log(3.0)))


def draw_q_gain(key, part):
    return gain_helper(jax.random.fold_in(key, 11))


def draw_k_gain(key, part):
    return gain_helper(jax.random.fold_in(key, 12))


def draw_counts(key, part):
    key = jax.random.fold_in(key, 14)
    first, second, third = jax.random.split(key, 3)
    values = jax.random.randint(first, (NBLK,), 0, LIST + 1, dtype=jnp.int32)
    half_blocks = NBLK // 2
    full_place = jax.random.randint(second, (), 0, half_blocks, dtype=jnp.int32)
    empty_place = half_blocks + jax.random.randint(third, (), 0, NBLK - half_blocks, dtype=jnp.int32)
    values = values.at[full_place].set(LIST)
    values = values.at[empty_place].set(0)
    return values


def plant(values, own_key, smallest, top_value):
    place = [jax.random.randint(jax.random.fold_in(own_key, axis), (), 0, length) for axis, length in enumerate(values.shape)]
    main_axis = values.shape.index(max(values.shape))
    next_to = place[:main_axis] + [(place[main_axis] + 1) % values.shape[main_axis]] + place[main_axis + 1:]
    return values.at[tuple(place)].set(smallest).at[tuple(next_to)].set(top_value)


def block_levels(stream_key, shape, pieces, low, high):
    loudness, own = 1.0, jax.random.fold_in(stream_key, 6)
    for position, parts in pieces:
        draws = jnp.exp(jax.random.uniform(jax.random.fold_in(own, position), (parts,), jnp.float32, low / len(pieces), high / len(pieces)))
        loudness = loudness * jnp.repeat(draws, shape[position] // parts).reshape([-1 if axis == position else 1 for axis in range(len(shape))])
    return loudness


def noise(own_key, extent, width, bound, shards=(), kind=jnp.bfloat16):
    level = block_levels(own_key, extent, shards, -0.22, 0.18) if shards else 1.0
    drawn = jax.random.normal(own_key, extent, jnp.float32) * width * level
    return jnp.minimum(jnp.maximum(drawn, -bound), bound).astype(kind)


def setup_inputs(seed: int = 0) -> dict:
    key_list = jax.random.split(jax.random.key(seed), 12)
    return {
        "text_states": draw_text_states(jax.random.fold_in(key_list[11], 71), 0),
        "text_gain": jnp.clip(1.0 + 0.18 * jax.random.normal(key_list[1], (D,), jnp.float32), 0.1, 1.9),
        "vision": noise(key_list[2], (IMAGES, VIS, D), 1.0, 6.0, ((0, 2), (1, 16))),
        "q_weight": noise(key_list[3], (D, QHEADS * HD), D ** -0.5, 0.0625, ((0, 16), (1, 2))),
        "k_weight": noise(key_list[4], (D, KVH * HD), D ** -0.5, 0.0625, ((0, 16), (1, 2))),
        "v_weight": noise(key_list[5], (D, KVH * HD), D ** -0.5, 0.0625, ((0, 16), (1, 2))),
        "q_gain": draw_q_gain(jax.random.fold_in(key_list[11], 71), 0),
        "k_gain": draw_k_gain(jax.random.fold_in(key_list[11], 71), 0),
        "owners": plant(jax.random.randint(key_list[8], (NBLK, LIST), 0, IMAGES), jax.random.fold_in(key_list[8], 1), 0, IMAGES - 1).astype(jnp.int32),
        "counts": draw_counts(jax.random.fold_in(key_list[11], 71), 0),
        "gate_value": jnp.clip(jax.random.uniform(key_list[10], (1,), jnp.float32, 0.3, 1.5), 0.3, 1.5),
    }


norm_epsilon = 1e-05
masked_score = -1e+30

def head_norm(values, gain):
    mean_square = lax.optimization_barrier(jnp.mean(values * values, axis=-1, keepdims=True))
    return values * lax.rsqrt(mean_square + norm_epsilon) * gain

def reference(text_states, text_gain, vision, q_weight, k_weight, v_weight, q_gain, k_gain, owners, counts, gate_value):
    text_float = text_states.astype(jnp.float32)
    normed = (text_float * lax.rsqrt(lax.optimization_barrier(jnp.mean(text_float * text_float, axis=-1, keepdims=True)) + norm_epsilon) * text_gain).astype(jnp.bfloat16)
    query_full = jnp.dot(normed, q_weight, preferred_element_type=jnp.float32)
    queries = head_norm(query_full.reshape(TOKENS, QHEADS, HD), q_gain).astype(jnp.bfloat16)
    visual = vision.reshape(IMAGES * VIS, D)
    key_full = jnp.dot(visual, k_weight, preferred_element_type=jnp.float32).reshape(IMAGES * VIS, KVH, HD)
    keys = head_norm(key_full, k_gain).astype(jnp.bfloat16)
    values = jnp.dot(visual, v_weight, preferred_element_type=jnp.float32).astype(jnp.bfloat16).reshape(IMAGES * VIS, KVH, HD)
    live_slot = jnp.arange(LIST, dtype=jnp.int32)[None, :] < counts[:, None]
    matched = (owners[:, :, None] == jnp.arange(IMAGES, dtype=jnp.int32)[None, None, :]) & live_slot[:, :, None]
    block_images = jnp.any(matched, axis=1)
    token_images = jnp.repeat(block_images, BLK, axis=0)
    key_allowed = jnp.repeat(token_images, VIS, axis=1)
    row_live = jnp.any(token_images, axis=1)
    score_scale = HD ** (-0.5)

    def one_head(head_index):
        group = head_index // QH_DEV
        query_head = queries[:, head_index, :]
        key_head = keys[:, group, :]
        value_head = values[:, group, :]
        scores = jnp.dot(query_head, key_head.T, preferred_element_type=jnp.float32) * score_scale
        scores = jnp.where(key_allowed, scores, masked_score)
        highest = lax.optimization_barrier(jnp.max(scores, axis=1, keepdims=True))
        weights = jnp.exp(scores - highest).astype(jnp.bfloat16)
        denominator = lax.optimization_barrier(jnp.sum(weights.astype(jnp.float32), axis=1, keepdims=True))
        numerator = jnp.dot(weights, value_head, preferred_element_type=jnp.float32)
        return numerator / denominator
    heads = lax.map(one_head, jnp.arange(QHEADS, dtype=jnp.int32))
    factor = jnp.where(row_live, jnp.tanh(gate_value[0]), jnp.float32(0.0))
    gated = heads * factor[None, :, None]
    return jnp.transpose(gated, (1, 0, 2)).reshape(TOKENS, QHEADS * HD).astype(jnp.bfloat16)
```

```python
import functools

import jax
import jax.numpy as jnp
from jax import lax
from jax.experimental import pallas as pl
from jax.experimental.pallas import tpu as pltpu
from jax.sharding import PartitionSpec as P

norm_epsilon = 1e-05
masked_score = -1e30
MESH = pl.DeviceIdType.MESH
row_tile = 16


def head_norm(values, gain):
    mean_square = jnp.mean(values * values, axis=-1, keepdims=True)
    return values * lax.rsqrt(mean_square + norm_epsilon) * gain


def kernel(
    images, shards, group, halves,
    text_ref, gain_ref, vision_ref, q_ref, k_ref, v_ref, qg_ref, kg_ref, owners_ref, counts_ref, gate_ref,
    out_ref,
    normed, others, wbuf, total, part_send, part_recv,
    vis_send, vis_all, pair_send, pair_recv, kv_own, kv_all,
    w_send, w_recv, t_send, t_recv, f_send, f_recv, p_send, p_recv, v_send, v_recv, s_send, s_recv,
):
    img = lax.axis_index("img")
    me = lax.axis_index("fsdp")
    line = shards // group
    along = lax.div(me, group)
    member = lax.rem(me, group)
    rows, width = text_ref.shape
    depth, columns = q_ref.shape
    half = columns // halves
    head = qg_ref.shape[1]
    tokens = vision_ref.shape[1]
    part_rows = rows // images

    def copy(src, dst, send, recv, target):
        return pltpu.make_async_remote_copy(
            src_ref=src, dst_ref=dst, send_sem=send, recv_sem=recv, device_id=target, device_id_type=MESH
        )

    def drain(ref, sem):
        pltpu.make_async_copy(ref, ref, sem).wait()

    barrier = pltpu.get_barrier_semaphore()

    def greet(step, carry):
        pl.semaphore_signal(barrier, inc=1, device_id={"fsdp": lax.rem(me + step, shards)}, device_id_type=MESH)
        return carry

    lax.fori_loop(1, shards, greet, 0)
    for j in range(1, images):
        pl.semaphore_signal(barrier, inc=1, device_id={"img": lax.rem(img + j, images)}, device_id_type=MESH)
    for h in range(halves):
        wbuf[h, along] = q_ref[:, h * half : (h + 1) * half]
    for f in range(shards):
        vis_send[f] = vision_ref[0, :, f * depth : (f + 1) * depth].astype(jnp.float32)
    vis_all[img, me] = vis_send[me]
    pl.semaphore_wait(barrier, shards - 1 + images - 1)

    def w_copy(h, step, way):
        slot = along - step if way == 0 else along + step
        to = me + group if way == 0 else me - group
        return copy(
            wbuf.at[h, slot], wbuf.at[h, slot], w_send.at[h, step, way], w_recv.at[h, step, way], {"fsdp": to}
        )

    def w_sends(step, way):
        if way == 0:
            return (along - step >= 0) & (along + 1 < line)
        return (along + step < line) & (along >= 1)

    def w_gets(step, way):
        if way == 0:
            return along - 1 - step >= 0
        return along + 1 + step < line

    def w_start(h, step):
        for way in range(2):
            @pl.when(w_sends(step, way))
            def _():
                w_copy(h, step, way).start()

    def w_arrive(h, step):
        for way in range(2):
            @pl.when(w_gets(step, way))
            def _():
                w_copy(h, step, way).wait_recv()
        if step + 1 < line - 1:
            w_start(h, step + 1)

    def spread(source, target, send, recv):
        def one(step, carry):
            to = lax.rem(me + step, shards)
            copy(source(to), target, send, recv, {"fsdp": to}).start()
            return carry

        lax.fori_loop(1, shards, one, 0)

    w_start(0, 0)
    spread(lambda to: vis_send.at[to], vis_all.at[img, me], v_send.at[0], v_recv.at[0])

    def scale_of(row):
        acc = jnp.zeros((row_tile, depth), jnp.float32)
        for f in range(shards):
            x = text_ref[pl.ds(row, row_tile), f * depth : (f + 1) * depth].astype(jnp.float32)
            acc = acc + x * x
        return lax.rsqrt(jnp.sum(acc, axis=1, keepdims=True) / width + norm_epsilon)

    def norm_all(t, carry):
        row = pl.multiple_of(img * part_rows + t * row_tile, row_tile)
        scale = scale_of(row)
        for f in range(shards):
            span = slice(f * depth, (f + 1) * depth)
            x = text_ref[pl.ds(row, row_tile), span].astype(jnp.float32)
            place = f // group * depth
            normed[f % group, pl.ds(row, row_tile), place : place + depth] = (x * scale * gain_ref[:, span]).astype(
                jnp.bfloat16
            )
        return carry

    lax.fori_loop(0, part_rows // row_tile, norm_all, 0)
    mine = pl.ds(pl.multiple_of(img * part_rows, part_rows), part_rows)

    def t_copy(d):
        to = lax.rem(member + d, group)
        return copy(
            normed.at[to, mine], others.at[d - 1, mine], t_send.at[d - 1], t_recv.at[d - 1],
            {"fsdp": along * group + to},
        )

    for d in range(1, group):
        t_copy(d).start()

    for j in range(1, images):
        def norm_own(t, carry):
            row = pl.multiple_of(lax.rem(img + j, images) * part_rows + t * row_tile, row_tile)
            scale = scale_of(row)
            for a in range(line):
                span = pl.ds(pl.multiple_of((a * group + member) * depth, depth), depth)
                x = text_ref[pl.ds(row, row_tile), span].astype(jnp.float32)
                normed[member, pl.ds(row, row_tile), a * depth : (a + 1) * depth] = (
                    x * scale * gain_ref[:, span]
                ).astype(jnp.bfloat16)
            return carry

        lax.fori_loop(0, part_rows // row_tile, norm_own, 0)

    drain(vis_all.at[img, pl.ds(0, shards - 1)], v_recv.at[0])

    def s_copy(j):
        return copy(
            vis_all.at[img], vis_all.at[img], s_send.at[j - 1], s_recv.at[j - 1], {"img": lax.rem(img + j, images)}
        )

    for j in range(1, images):
        s_copy(j).start()
    w_arrive(0, 0)
    w_start(1, 0)
    for j in range(1, images):
        s_copy(j).wait_recv()
    for m in range(images):
        x = vis_all[m].reshape(shards * tokens, depth).astype(jnp.bfloat16)
        keys_part = jnp.dot(x, k_ref[...], preferred_element_type=jnp.float32)
        values_part = jnp.dot(x, v_ref[...], preferred_element_type=jnp.float32)
        pair_send[:, m, :, :head] = keys_part.reshape(shards, tokens, head)
        pair_send[:, m, :, head:] = values_part.reshape(shards, tokens, head)
    spread(lambda to: pair_send.at[to], pair_recv.at[me], v_send.at[1], v_recv.at[1])
    pair_recv[me] = pair_send[me]
    for step in range(1, line - 1):
        w_arrive(0, step)
        if step == 1:
            drain(pair_recv.at[pl.ds(0, shards - 1)], v_recv.at[1])
            pair = jnp.sum(pair_recv[...], axis=0).reshape(images * tokens, 2 * head)
            kv_own[:, :head] = head_norm(pair[:, :head], kg_ref[...]).astype(jnp.bfloat16)
            kv_own[:, head:] = pair[:, head:].astype(jnp.bfloat16)
            spread(lambda to: kv_own, kv_all.at[me], v_send.at[2], v_recv.at[2])
            kv_all[me] = kv_own[...]
    w_arrive(1, 0)

    def f_copy(d, j):
        return copy(
            others.at[d - 1, mine], others.at[d - 1, mine], f_send.at[d - 1, j - 1], f_recv.at[d - 1, j - 1],
            {"img": lax.rem(img + j, images)},
        )

    for d in range(1, group):
        t_copy(d).wait_recv()
        for j in range(1, images):
            f_copy(d, j).start()
    for d in range(1, group):
        for j in range(1, images):
            f_copy(d, j).wait_recv()

    def p_copy(h, d):
        to = lax.rem(member + group - d, group)
        return copy(
            part_send.at[h, d - 1], part_recv.at[h, d - 1], p_send.at[h, d - 1], p_recv.at[h, d - 1],
            {"fsdp": along * group + to},
        )

    def project(h):
        weight = wbuf[h].reshape(line * depth, half)
        for d in range(1, group):
            part_send[h, d - 1] = jnp.dot(others[d - 1], weight, preferred_element_type=jnp.float32)
            p_copy(h, d).start()
        total[h] = jnp.dot(normed[member], weight, preferred_element_type=jnp.float32)

    project(0)
    for step in range(1, line - 1):
        w_arrive(1, step)
    project(1)

    drain(kv_all.at[pl.ds(0, shards - 1)], v_recv.at[2])
    key_count = shards * images * tokens
    blocks = owners_ref.shape[0]
    key_image = lax.rem(lax.div(lax.broadcasted_iota(jnp.int32, (1, key_count), 1), tokens), images)
    gate = jnp.tanh(gate_ref[...])
    masks, factors = [], []
    for blk in range(blocks):
        row = jnp.zeros((1, key_count), jnp.int32)
        live = jnp.int32(0)
        for m in range(images):
            hit = jnp.int32(0)
            for slot in range(owners_ref.shape[1]):
                same = jnp.where(owners_ref[blk, slot] == m, 1, 0)
                hit = jnp.maximum(hit, jnp.where(slot < counts_ref[blk], same, 0))
            row = jnp.where(key_image == m, hit, row)
            live = jnp.maximum(live, hit)
        masks.append(jnp.broadcast_to(row, (rows // blocks, key_count)))
        factors.append(jnp.broadcast_to(gate * live.astype(jnp.float32), (rows // blocks, 1)))
    allowed = jnp.concatenate(masks, axis=0) > 0
    factor = jnp.concatenate(factors, axis=0)
    pairs = kv_all[...].reshape(key_count, 2 * head)
    keys, values = pairs[:, :head], pairs[:, head:]
    for h in range(halves):
        for d in range(1, group):
            p_copy(h, d).wait_recv()
        full = total[h]
        for d in range(1, group):
            full = full + part_recv[h, d - 1]
        for n in range(half // head):
            queries = head_norm(full[:, n * head : (n + 1) * head], qg_ref[...]).astype(jnp.bfloat16)
            scores = lax.dot_general(
                queries, keys, (((1,), (1,)), ((), ())), preferred_element_type=jnp.float32
            ) * head ** (-0.5)
            scores = jnp.where(allowed, scores, masked_score)
            weights = jnp.exp(scores - jnp.max(scores, axis=1, keepdims=True)).astype(jnp.bfloat16)
            denominator = jnp.sum(weights.astype(jnp.float32), axis=1, keepdims=True)
            numerator = jnp.dot(weights, values, preferred_element_type=jnp.float32)
            place = h * half + n * head
            out_ref[:, place : place + head] = (numerator / denominator * factor).astype(jnp.bfloat16)

    for h in range(halves):
        for step in range(line - 1):
            for way in range(2):
                @pl.when(w_sends(step, way))
                def _():
                    w_copy(h, step, way).wait_send()
        for d in range(1, group):
            p_copy(h, d).wait_send()
    for d in range(1, group):
        t_copy(d).wait_send()
        for j in range(1, images):
            f_copy(d, j).wait_send()
    for j in range(1, images):
        s_copy(j).wait_send()
    drain(vis_send.at[pl.ds(0, shards - 1)], v_send.at[0])
    drain(pair_send.at[pl.ds(0, shards - 1)], v_send.at[1])
    drain(kv_all.at[pl.ds(0, shards - 1)], v_send.at[2])


def on_device(
    text_states, text_gain, vision, q_weight, k_weight, v_weight, q_gain, k_gain, owners, counts, gate_value,
):
    images = lax.axis_size("img")
    shards = lax.axis_size("fsdp")
    group, halves = 4, 2
    line = shards // group
    rows, width = text_states.shape
    depth, columns = q_weight.shape
    half = columns // halves
    tokens = vision.shape[1]
    head = q_gain.shape[0]
    bf16, f32 = jnp.bfloat16, jnp.float32
    vmem = pl.BlockSpec(memory_space=pltpu.VMEM)
    smem = pl.BlockSpec(memory_space=pltpu.SMEM)
    dma = pltpu.SemaphoreType.DMA
    return pl.pallas_call(
        functools.partial(kernel, images, shards, group, halves),
        out_shape=jax.ShapeDtypeStruct((rows, columns), bf16),
        in_specs=[vmem] * 8 + [smem, smem, vmem],
        out_specs=vmem,
        scratch_shapes=[
            pltpu.VMEM((group, rows, line * depth), bf16),
            pltpu.VMEM((group - 1, rows, line * depth), bf16),
            pltpu.VMEM((halves, line, depth, half), bf16),
            pltpu.VMEM((halves, rows, half), f32),
            pltpu.VMEM((halves, group - 1, rows, half), f32),
            pltpu.VMEM((halves, group - 1, rows, half), f32),
            pltpu.VMEM((shards, tokens, depth), f32),
            pltpu.VMEM((images, shards, tokens, depth), f32),
            pltpu.VMEM((shards, images, tokens, 2 * head), f32),
            pltpu.VMEM((shards, images, tokens, 2 * head), f32),
            pltpu.VMEM((images * tokens, 2 * head), bf16),
            pltpu.VMEM((shards, images * tokens, 2 * head), bf16),
            dma((halves, line - 1, 2)),
            dma((halves, line - 1, 2)),
            dma((group - 1,)),
            dma((group - 1,)),
            dma((group - 1, images - 1)),
            dma((group - 1, images - 1)),
            dma((halves, group - 1)),
            dma((halves, group - 1)),
            dma((3,)),
            dma((3,)),
            dma((images - 1,)),
            dma((images - 1,)),
        ],
        compiler_params=pltpu.CompilerParams(
            collective_id=0, has_side_effects=True, vmem_limit_bytes=56 * 2**20
        ),
    )(
        text_states, text_gain[None], vision, q_weight, k_weight, v_weight, q_gain[None], k_gain[None],
        owners, counts, gate_value[None],
    )


def solution(mesh):
    in_specs = (
        P("fsdp", None),
        P(),
        P("img", "fsdp", None),
        P("fsdp", "img"),
        P("fsdp", "img"),
        P("fsdp", "img"),
        P(),
        P(),
        P("fsdp", None),
        P("fsdp"),
        P(),
    )
    out_specs = P("fsdp", "img")
    return jax.shard_map(
        on_device, mesh=mesh, in_specs=in_specs, out_specs=out_specs, check_vma=False
    )
```

```python
import functools

import jax
import jax.numpy as jnp
from jax import lax
from jax.experimental import pallas as pl
from jax.experimental.pallas import tpu as pltpu
from jax.sharding import PartitionSpec as P

norm_epsilon = 1e-05
masked_score = -1e30
MESH = pl.DeviceIdType.MESH
row_tile = 16


def head_norm(values, gain):
    mean_square = jnp.mean(values * values, axis=-1, keepdims=True)
    return values * lax.rsqrt(mean_square + norm_epsilon) * gain


def kernel(
    images, shards, group, halves, pieces,
    text_hbm, gain_ref, vision_ref, q_ref, k_ref, v_ref, qg_ref, kg_ref, owners_ref, counts_ref, gate_ref,
    out_ref,
    text_ref, normed, others, wbuf, total, part_send, part_recv,
    vis_send, vis_all, pair_send, pair_recv, kv_own, kv_all,
    w_send, w_recv, t_send, t_recv, f_send, f_recv, p_send, p_recv, v_send, v_recv, s_send, s_recv, load,
):
    img = lax.axis_index("img")
    me = lax.axis_index("fsdp")
    line = shards // group
    along = lax.div(me, group)
    member = lax.rem(me, group)
    rows, width = text_hbm.shape
    depth, columns = q_ref.shape
    half = columns // halves
    head = qg_ref.shape[1]
    tokens = vision_ref.shape[1]
    part_rows = rows // images
    piece_rows = part_rows // pieces

    def copy(src, dst, send, recv, target):
        return pltpu.make_async_remote_copy(
            src_ref=src, dst_ref=dst, send_sem=send, recv_sem=recv, device_id=target, device_id_type=MESH
        )

    def drain(ref, sem):
        pltpu.make_async_copy(ref, ref, sem).wait()

    barrier = pltpu.get_barrier_semaphore()

    def greet(step, carry):
        pl.semaphore_signal(barrier, inc=1, device_id={"fsdp": lax.rem(me + step, shards)}, device_id_type=MESH)
        return carry

    lax.fori_loop(1, shards, greet, 0)
    for j in range(1, images):
        pl.semaphore_signal(barrier, inc=1, device_id={"img": lax.rem(img + j, images)}, device_id_type=MESH)
    def t_load(j):
        span = pl.ds(pl.multiple_of(lax.rem(img + j, images) * part_rows, part_rows), part_rows)
        return pltpu.make_async_copy(text_hbm.at[span], text_ref.at[span], load.at[j])

    for j in range(images):
        t_load(j).start()
    for h in range(halves):
        wbuf[h, along] = q_ref[:, h * half : (h + 1) * half]
    for f in range(shards):
        vis_send[f] = vision_ref[0, :, f * depth : (f + 1) * depth].astype(jnp.float32)
    vis_all[img, me] = vis_send[me]
    pl.semaphore_wait(barrier, shards - 1 + images - 1)

    def w_copy(h, step, way):
        slot = along - step if way == 0 else along + step
        to = me + group if way == 0 else me - group
        return copy(
            wbuf.at[h, slot], wbuf.at[h, slot], w_send.at[h, step, way], w_recv.at[h, step, way], {"fsdp": to}
        )

    def w_sends(step, way):
        if way == 0:
            return (along - step >= 0) & (along + 1 < line)
        return (along + step < line) & (along >= 1)

    def w_gets(step, way):
        if way == 0:
            return along - 1 - step >= 0
        return along + 1 + step < line

    def w_start(h, step):
        for way in range(2):
            @pl.when(w_sends(step, way))
            def _():
                w_copy(h, step, way).start()

    def w_arrive(h, step):
        for way in range(2):
            @pl.when(w_gets(step, way))
            def _():
                w_copy(h, step, way).wait_recv()
        if step + 1 < line - 1:
            w_start(h, step + 1)

    def spread(source, target, send, recv):
        def one(step, carry):
            to = lax.rem(me + step, shards)
            copy(source(to), target, send, recv, {"fsdp": to}).start()
            return carry

        lax.fori_loop(1, shards, one, 0)

    w_start(0, 0)
    spread(lambda to: vis_send.at[to], vis_all.at[img, me], v_send.at[0], v_recv.at[0])

    def scale_of(row):
        acc = jnp.zeros((row_tile, depth), jnp.float32)
        for f in range(shards):
            x = text_ref[pl.ds(row, row_tile), f * depth : (f + 1) * depth].astype(jnp.float32)
            acc = acc + x * x
        return lax.rsqrt(jnp.sum(acc, axis=1, keepdims=True) / width + norm_epsilon)

    def norm_all(t, carry):
        row = pl.multiple_of(img * part_rows + t * row_tile, row_tile)
        scale = scale_of(row)
        for f in range(shards):
            span = slice(f * depth, (f + 1) * depth)
            x = text_ref[pl.ds(row, row_tile), span].astype(jnp.float32)
            place = f // group * depth
            normed[f % group, pl.ds(row, row_tile), place : place + depth] = (x * scale * gain_ref[:, span]).astype(
                jnp.bfloat16
            )
        return carry

    def partner(d):
        low = lax.rem(lax.rem(member, 2) + d % 2, 2)
        high = lax.rem(lax.div(member, 2) + d // 2, 2)
        return high * 2 + low

    def piece(t):
        return pl.ds(pl.multiple_of(img * part_rows + t * piece_rows, piece_rows), piece_rows)

    def t_copy(d, t):
        to = partner(d)
        return copy(
            normed.at[to, piece(t)], others.at[d - 1, piece(t)], t_send.at[d - 1, t], t_recv.at[d - 1, t],
            {"fsdp": along * group + to},
        )

    t_load(0).wait()
    steps = piece_rows // row_tile
    for t in range(pieces):
        lax.fori_loop(t * steps, (t + 1) * steps, norm_all, 0)
        for d in range(1, group):
            t_copy(d, t).start()

    for j in range(1, images):
        t_load(j).wait()

        def norm_own(t, carry):
            row = pl.multiple_of(lax.rem(img + j, images) * part_rows + t * row_tile, row_tile)
            scale = scale_of(row)
            for a in range(line):
                span = pl.ds(pl.multiple_of((a * group + member) * depth, depth), depth)
                x = text_ref[pl.ds(row, row_tile), span].astype(jnp.float32)
                normed[member, pl.ds(row, row_tile), a * depth : (a + 1) * depth] = (
                    x * scale * gain_ref[:, span]
                ).astype(jnp.bfloat16)
            return carry

        lax.fori_loop(0, part_rows // row_tile, norm_own, 0)

    drain(vis_all.at[img, pl.ds(0, shards - 1)], v_recv.at[0])

    def s_copy(j):
        return copy(
            vis_all.at[img], vis_all.at[img], s_send.at[j - 1], s_recv.at[j - 1], {"img": lax.rem(img + j, images)}
        )

    for j in range(1, images):
        s_copy(j).start()
    w_arrive(0, 0)
    w_start(1, 0)
    for j in range(1, images):
        s_copy(j).wait_recv()
    for m in range(images):
        x = vis_all[m].reshape(shards * tokens, depth).astype(jnp.bfloat16)
        keys_part = jnp.dot(x, k_ref[...], preferred_element_type=jnp.float32)
        values_part = jnp.dot(x, v_ref[...], preferred_element_type=jnp.float32)
        pair_send[:, m, :, :head] = keys_part.reshape(shards, tokens, head)
        pair_send[:, m, :, head:] = values_part.reshape(shards, tokens, head)
    spread(lambda to: pair_send.at[to], pair_recv.at[me], v_send.at[1], v_recv.at[1])
    pair_recv[me] = pair_send[me]
    for step in range(1, line - 1):
        w_arrive(0, step)
    w_arrive(1, 0)

    def f_copy(d, t, j):
        return copy(
            others.at[d - 1, piece(t)], others.at[d - 1, piece(t)],
            f_send.at[d - 1, t, j - 1], f_recv.at[d - 1, t, j - 1], {"img": lax.rem(img + j, images)},
        )

    def t_arrive(d):
        for t in range(pieces):
            t_copy(d, t).wait_recv()
            for j in range(1, images):
                f_copy(d, t, j).start()

    def f_arrive(d):
        for t in range(pieces):
            for j in range(1, images):
                f_copy(d, t, j).wait_recv()

    def p_copy(h, d):
        return copy(
            part_send.at[h, d - 1], part_recv.at[h, d - 1], p_send.at[h, d - 1], p_recv.at[h, d - 1],
            {"fsdp": along * group + partner(d)},
        )

    def project(h, d):
        weight = wbuf[h].reshape(line * depth, half)
        product = jnp.dot(
            normed[member] if d == 0 else others[d - 1], weight, preferred_element_type=jnp.float32
        )
        if d == 0:
            total[h] = product
        else:
            part_send[h, d - 1] = product.astype(part_send.dtype)
            p_copy(h, d).start()

    t_arrive(1)
    t_arrive(2)
    f_arrive(1)
    project(0, 1)
    f_arrive(2)
    project(0, 2)
    w_arrive(1, 1)
    t_arrive(3)
    f_arrive(3)
    project(0, 3)
    drain(pair_recv.at[pl.ds(0, shards - 1)], v_recv.at[1])
    pair = jnp.sum(pair_recv[...], axis=0).reshape(images * tokens, 2 * head)
    kv_own[:, :head] = head_norm(pair[:, :head], kg_ref[...]).astype(jnp.bfloat16)
    kv_own[:, head:] = pair[:, head:].astype(jnp.bfloat16)
    spread(lambda to: kv_own, kv_all.at[me], v_send.at[2], v_recv.at[2])
    kv_all[me] = kv_own[...]
    project(0, 0)
    for step in range(2, line - 1):
        w_arrive(1, step)
    for d in range(1, group):
        project(1, d)
    project(1, 0)

    drain(kv_all.at[pl.ds(0, shards - 1)], v_recv.at[2])
    key_count = shards * images * tokens
    blocks = owners_ref.shape[0]
    key_image = lax.rem(lax.div(lax.broadcasted_iota(jnp.int32, (1, key_count), 1), tokens), images)
    gate = jnp.tanh(gate_ref[...])
    masks, factors = [], []
    for blk in range(blocks):
        row = jnp.zeros((1, key_count), jnp.int32)
        live = jnp.int32(0)
        for m in range(images):
            hit = jnp.int32(0)
            for slot in range(owners_ref.shape[1]):
                same = jnp.where(owners_ref[blk, slot] == m, 1, 0)
                hit = jnp.maximum(hit, jnp.where(slot < counts_ref[blk], same, 0))
            row = jnp.where(key_image == m, hit, row)
            live = jnp.maximum(live, hit)
        masks.append(jnp.broadcast_to(row, (rows // blocks, key_count)))
        factors.append(jnp.broadcast_to(gate * live.astype(jnp.float32), (rows // blocks, 1)))
    allowed = jnp.concatenate(masks, axis=0) > 0
    factor = jnp.concatenate(factors, axis=0)
    pairs = kv_all[...].reshape(key_count, 2 * head)
    keys, values = pairs[:, :head], pairs[:, head:]
    for h in range(halves):
        for d in range(1, group):
            p_copy(h, d).wait_recv()
        full = total[h]
        for d in range(1, group):
            full = full + part_recv[h, d - 1].astype(jnp.float32)
        for n in range(half // head):
            queries = head_norm(full[:, n * head : (n + 1) * head], qg_ref[...]).astype(jnp.bfloat16)
            scores = lax.dot_general(
                queries, keys, (((1,), (1,)), ((), ())), preferred_element_type=jnp.float32
            ) * head ** (-0.5)
            scores = jnp.where(allowed, scores, masked_score)
            weights = jnp.exp(scores - jnp.max(scores, axis=1, keepdims=True)).astype(jnp.bfloat16)
            denominator = jnp.sum(weights.astype(jnp.float32), axis=1, keepdims=True)
            numerator = jnp.dot(weights, values, preferred_element_type=jnp.float32)
            place = h * half + n * head
            out_ref[:, place : place + head] = (numerator / denominator * factor).astype(jnp.bfloat16)

    for h in range(halves):
        for step in range(line - 1):
            for way in range(2):
                @pl.when(w_sends(step, way))
                def _():
                    w_copy(h, step, way).wait_send()
        for d in range(1, group):
            p_copy(h, d).wait_send()
    for d in range(1, group):
        for t in range(pieces):
            t_copy(d, t).wait_send()
            for j in range(1, images):
                f_copy(d, t, j).wait_send()
    for j in range(1, images):
        s_copy(j).wait_send()
    drain(vis_send.at[pl.ds(0, shards - 1)], v_send.at[0])
    drain(pair_send.at[pl.ds(0, shards - 1)], v_send.at[1])
    drain(kv_all.at[pl.ds(0, shards - 1)], v_send.at[2])


def on_device(
    text_states, text_gain, vision, q_weight, k_weight, v_weight, q_gain, k_gain, owners, counts, gate_value,
):
    images = lax.axis_size("img")
    shards = lax.axis_size("fsdp")
    group, halves, pieces = 4, 2, 2
    line = shards // group
    rows, width = text_states.shape
    depth, columns = q_weight.shape
    half = columns // halves
    tokens = vision.shape[1]
    head = q_gain.shape[0]
    bf16, f32 = jnp.bfloat16, jnp.float32
    vmem = pl.BlockSpec(memory_space=pltpu.VMEM)
    smem = pl.BlockSpec(memory_space=pltpu.SMEM)
    dma = pltpu.SemaphoreType.DMA
    return pl.pallas_call(
        functools.partial(kernel, images, shards, group, halves, pieces),
        out_shape=jax.ShapeDtypeStruct((rows, columns), bf16),
        in_specs=[pl.BlockSpec(memory_space=pl.ANY)] + [vmem] * 7 + [smem, smem, vmem],
        out_specs=vmem,
        scratch_shapes=[
            pltpu.VMEM((rows, width), bf16),
            pltpu.VMEM((group, rows, line * depth), bf16),
            pltpu.VMEM((group - 1, rows, line * depth), bf16),
            pltpu.VMEM((halves, line, depth, half), bf16),
            pltpu.VMEM((halves, rows, half), f32),
            pltpu.VMEM((halves, group - 1, rows, half), f32),
            pltpu.VMEM((halves, group - 1, rows, half), f32),
            pltpu.VMEM((shards, tokens, depth), f32),
            pltpu.VMEM((images, shards, tokens, depth), f32),
            pltpu.VMEM((shards, images, tokens, 2 * head), f32),
            pltpu.VMEM((shards, images, tokens, 2 * head), f32),
            pltpu.VMEM((images * tokens, 2 * head), bf16),
            pltpu.VMEM((shards, images * tokens, 2 * head), bf16),
            dma((halves, line - 1, 2)),
            dma((halves, line - 1, 2)),
            dma((group - 1, pieces)),
            dma((group - 1, pieces)),
            dma((group - 1, pieces, images - 1)),
            dma((group - 1, pieces, images - 1)),
            dma((halves, group - 1)),
            dma((halves, group - 1)),
            dma((3,)),
            dma((3,)),
            dma((images - 1,)),
            dma((images - 1,)),
            dma((images,)),
        ],
        compiler_params=pltpu.CompilerParams(
            collective_id=0, has_side_effects=True, vmem_limit_bytes=56 * 2**20
        ),
    )(
        text_states, text_gain[None], vision, q_weight, k_weight, v_weight, q_gain[None], k_gain[None],
        owners, counts, gate_value[None],
    )


def solution(mesh):
    in_specs = (
        P("fsdp", None),
        P(),
        P("img", "fsdp", None),
        P("fsdp", "img"),
        P("fsdp", "img"),
        P("fsdp", "img"),
        P(),
        P(),
        P("fsdp", None),
        P("fsdp"),
        P(),
    )
    out_specs = P("fsdp", "img")
    return jax.shard_map(
        on_device, mesh=mesh, in_specs=in_specs, out_specs=out_specs, check_vma=False
    )
```

```python
import functools

import jax
import jax.numpy as jnp
from jax import lax
from jax.experimental import pallas as pl
from jax.experimental.pallas import tpu as pltpu
from jax.sharding import PartitionSpec as P

norm_epsilon = 1e-05
masked_score = -1e30
MESH = pl.DeviceIdType.MESH
row_tile = 16


def head_norm(values, gain):
    mean_square = jnp.mean(values * values, axis=-1, keepdims=True)
    return values * lax.rsqrt(mean_square + norm_epsilon) * gain


def kernel(
    images, shards, group, halves, pieces,
    text_hbm, gain_ref, vision_ref, q_ref, k_ref, v_ref, qg_ref, kg_ref, owners_ref, counts_ref, gate_ref,
    out_ref,
    text_ref, normed, others, wbuf, total, part_send, part_recv,
    vis_send, vis_all, pair_send, pair_recv, pair_plane, pair_near, kv_own, kv_all,
    w_send, w_recv, t_send, t_recv, f_send, f_recv, p_send, p_recv, v_send, v_recv, s_send, s_recv, load,
):
    img = lax.axis_index("img")
    me = lax.axis_index("fsdp")
    line = shards // group
    along = lax.div(me, group)
    member = lax.rem(me, group)
    rows, width = text_hbm.shape
    depth, columns = q_ref.shape
    half = columns // halves
    head = qg_ref.shape[1]
    tokens = vision_ref.shape[1]
    part_rows = rows // images
    piece_rows = part_rows // pieces

    def copy(src, dst, send, recv, target):
        return pltpu.make_async_remote_copy(
            src_ref=src, dst_ref=dst, send_sem=send, recv_sem=recv, device_id=target, device_id_type=MESH
        )

    def drain(ref, sem):
        pltpu.make_async_copy(ref, ref, sem).wait()

    barrier = pltpu.get_barrier_semaphore()

    def greet(step, carry):
        pl.semaphore_signal(barrier, inc=1, device_id={"fsdp": lax.rem(me + step, shards)}, device_id_type=MESH)
        return carry

    lax.fori_loop(1, shards, greet, 0)
    for j in range(1, images):
        pl.semaphore_signal(barrier, inc=1, device_id={"img": lax.rem(img + j, images)}, device_id_type=MESH)
    def t_load(j):
        span = pl.ds(pl.multiple_of(lax.rem(img + j, images) * part_rows, part_rows), part_rows)
        return pltpu.make_async_copy(text_hbm.at[span], text_ref.at[span], load.at[j])

    for j in range(images):
        t_load(j).start()
    for h in range(halves):
        wbuf[h, along] = q_ref[:, h * half : (h + 1) * half]
    for f in range(shards):
        vis_send[f] = vision_ref[0, :, f * depth : (f + 1) * depth].astype(jnp.float32)
    vis_all[img, me] = vis_send[me]
    pl.semaphore_wait(barrier, shards - 1 + images - 1)

    def w_copy(h, step, way):
        slot = along - step if way == 0 else along + step
        to = me + group if way == 0 else me - group
        return copy(
            wbuf.at[h, slot], wbuf.at[h, slot], w_send.at[h, step, way], w_recv.at[h, step, way], {"fsdp": to}
        )

    def w_sends(step, way):
        if way == 0:
            return (along - step >= 0) & (along + 1 < line)
        return (along + step < line) & (along >= 1)

    def w_gets(step, way):
        if way == 0:
            return along - 1 - step >= 0
        return along + 1 + step < line

    def w_start(h, step):
        for way in range(2):
            @pl.when(w_sends(step, way))
            def _():
                w_copy(h, step, way).start()

    def w_arrive(h, step):
        for way in range(2):
            @pl.when(w_gets(step, way))
            def _():
                w_copy(h, step, way).wait_recv()
        if step + 1 < line - 1:
            w_start(h, step + 1)

    def spread(source, target, send, recv):
        def one(step, carry):
            to = lax.rem(me + step, shards)
            copy(source(to), target, send, recv, {"fsdp": to}).start()
            return carry

        lax.fori_loop(1, shards, one, 0)

    w_start(0, 0)
    spread(lambda to: vis_send.at[to], vis_all.at[img, me], v_send.at[0], v_recv.at[0])

    def scale_of(row):
        acc = jnp.zeros((row_tile, depth), jnp.float32)
        for f in range(shards):
            x = text_ref[pl.ds(row, row_tile), f * depth : (f + 1) * depth].astype(jnp.float32)
            acc = acc + x * x
        return lax.rsqrt(jnp.sum(acc, axis=1, keepdims=True) / width + norm_epsilon)

    def norm_all(t, carry):
        row = pl.multiple_of(img * part_rows + t * row_tile, row_tile)
        scale = scale_of(row)
        for f in range(shards):
            span = slice(f * depth, (f + 1) * depth)
            x = text_ref[pl.ds(row, row_tile), span].astype(jnp.float32)
            place = f // group * depth
            normed[f % group, pl.ds(row, row_tile), place : place + depth] = (x * scale * gain_ref[:, span]).astype(
                jnp.bfloat16
            )
        return carry

    def partner(d):
        low = lax.rem(lax.rem(member, 2) + d % 2, 2)
        high = lax.rem(lax.div(member, 2) + d // 2, 2)
        return high * 2 + low

    def piece(t):
        return pl.ds(pl.multiple_of(img * part_rows + t * piece_rows, piece_rows), piece_rows)

    def t_copy(d, t):
        to = partner(d)
        return copy(
            normed.at[to, piece(t)], others.at[d - 1, piece(t)], t_send.at[d - 1, t], t_recv.at[d - 1, t],
            {"fsdp": along * group + to},
        )

    t_load(0).wait()
    steps = piece_rows // row_tile
    for t in range(pieces):
        lax.fori_loop(t * steps, (t + 1) * steps, norm_all, 0)
        for d in range(1, group):
            t_copy(d, t).start()

    for j in range(1, images):
        t_load(j).wait()

        def norm_own(t, carry):
            row = pl.multiple_of(lax.rem(img + j, images) * part_rows + t * row_tile, row_tile)
            scale = scale_of(row)
            for a in range(line):
                span = pl.ds(pl.multiple_of((a * group + member) * depth, depth), depth)
                x = text_ref[pl.ds(row, row_tile), span].astype(jnp.float32)
                normed[member, pl.ds(row, row_tile), a * depth : (a + 1) * depth] = (
                    x * scale * gain_ref[:, span]
                ).astype(jnp.bfloat16)
            return carry

        lax.fori_loop(0, part_rows // row_tile, norm_own, 0)

    drain(vis_all.at[img, pl.ds(0, shards - 1)], v_recv.at[0])

    def s_copy(j):
        return copy(
            vis_all.at[img], vis_all.at[img], s_send.at[j - 1], s_recv.at[j - 1], {"img": lax.rem(img + j, images)}
        )

    for j in range(1, images):
        s_copy(j).start()
    w_arrive(0, 0)
    w_start(1, 0)
    for j in range(1, images):
        s_copy(j).wait_recv()
    for m in range(images):
        x = vis_all[m].reshape(shards * tokens, depth).astype(jnp.bfloat16)
        keys_part = jnp.dot(x, k_ref[...], preferred_element_type=jnp.float32)
        values_part = jnp.dot(x, v_ref[...], preferred_element_type=jnp.float32)
        pair_send[:, :, m, :, :head] = keys_part.reshape(line, group, tokens, head)
        pair_send[:, :, m, :, head:] = values_part.reshape(line, group, tokens, head)

    def along_line(source, target, number):
        def one(step, carry):
            to = lax.rem(along + step, line)
            copy(source(to), target, v_send.at[number], v_recv.at[number], {"fsdp": to * group + member}).start()
            return carry

        lax.fori_loop(1, line, one, 0)

    def over_plane(source, target, number):
        for d in range(1, group):
            to = partner(d)
            copy(
                source(to), target(d), v_send.at[number], v_recv.at[number], {"fsdp": along * group + to}
            ).start()

    along_line(lambda to: pair_send.at[to], pair_recv.at[along], 1)
    pair_recv[along] = pair_send[along]
    for step in range(1, line - 1):
        w_arrive(0, step)
    drain(pair_recv.at[pl.ds(0, line - 1)], v_recv.at[1])
    pair_plane[...] = jnp.sum(pair_recv[...], axis=0)
    over_plane(lambda to: pair_plane.at[to], lambda d: pair_near.at[d - 1], 2)
    w_arrive(1, 0)

    def f_copy(d, t, j):
        return copy(
            others.at[d - 1, piece(t)], others.at[d - 1, piece(t)],
            f_send.at[d - 1, t, j - 1], f_recv.at[d - 1, t, j - 1], {"img": lax.rem(img + j, images)},
        )

    def t_arrive(d):
        for t in range(pieces):
            t_copy(d, t).wait_recv()
            for j in range(1, images):
                f_copy(d, t, j).start()

    def f_arrive(d):
        for t in range(pieces):
            for j in range(1, images):
                f_copy(d, t, j).wait_recv()

    def p_copy(h, c, number):
        first, second = (1, 2) if c == 0 else (2, 1)
        source = (first, 3, second)[number] - 1
        over = second if number == 2 else first
        return copy(
            part_send.at[h, c, source], part_recv.at[h, c, number], p_send.at[h, c, number],
            p_recv.at[h, c, number], {"fsdp": along * group + partner(over)},
        )

    lane = half // 2

    def project(h, d):
        weight = wbuf[h].reshape(line * depth, half)
        product = jnp.dot(
            normed[member] if d == 0 else others[d - 1], weight, preferred_element_type=jnp.float32
        )
        if d == 0:
            total[h] = product
            return
        for c in range(2):
            part_send[h, c, d - 1] = product[:, c * lane : (c + 1) * lane]
        if d == 3:
            p_copy(h, 0, 1).start()
            p_copy(h, 1, 1).start()
        else:
            p_copy(h, d - 1, 0).start()

    def relay(h):
        for c in range(2):
            p_copy(h, c, 1).wait_recv()
            second = 2 if c == 0 else 1
            part_send[h, c, second - 1] = part_send[h, c, second - 1] + part_recv[h, c, 1]
            p_copy(h, c, 2).start()

    t_arrive(1)
    t_arrive(2)
    f_arrive(1)
    project(0, 1)
    f_arrive(2)
    project(0, 2)
    w_arrive(1, 1)
    drain(pair_near, v_recv.at[2])
    pair = pair_plane[member]
    for d in range(1, group):
        pair = pair + pair_near[d - 1]
    pair = pair.reshape(images * tokens, 2 * head)
    kv_own[:, :head] = head_norm(pair[:, :head], kg_ref[...]).astype(jnp.bfloat16)
    kv_own[:, head:] = pair[:, head:].astype(jnp.bfloat16)
    over_plane(lambda to: kv_own, lambda d: kv_all.at[me], 3)
    kv_all[me] = kv_own[...]
    t_arrive(3)
    f_arrive(3)
    project(0, 3)
    project(0, 0)
    for step in range(2, line - 1):
        w_arrive(1, step)
    drain(kv_all.at[pl.ds(0, group - 1)], v_recv.at[3])
    plane = pl.ds(along * group, group)
    along_line(lambda to: kv_all.at[plane], kv_all.at[plane], 4)
    relay(0)
    for d in (3, 1, 2, 0):
        project(1, d)

    drain(kv_all.at[pl.ds(0, shards - group)], v_recv.at[4])
    key_count = shards * images * tokens
    blocks = owners_ref.shape[0]
    key_image = lax.rem(lax.div(lax.broadcasted_iota(jnp.int32, (1, key_count), 1), tokens), images)
    gate = jnp.tanh(gate_ref[...])
    masks, factors = [], []
    for blk in range(blocks):
        row = jnp.zeros((1, key_count), jnp.int32)
        live = jnp.int32(0)
        for m in range(images):
            hit = jnp.int32(0)
            for slot in range(owners_ref.shape[1]):
                same = jnp.where(owners_ref[blk, slot] == m, 1, 0)
                hit = jnp.maximum(hit, jnp.where(slot < counts_ref[blk], same, 0))
            row = jnp.where(key_image == m, hit, row)
            live = jnp.maximum(live, hit)
        masks.append(jnp.broadcast_to(row, (rows // blocks, key_count)))
        factors.append(jnp.broadcast_to(gate * live.astype(jnp.float32), (rows // blocks, 1)))
    allowed = jnp.concatenate(masks, axis=0) > 0
    factor = jnp.concatenate(factors, axis=0)
    pairs = kv_all[...].reshape(key_count, 2 * head)
    keys, values = pairs[:, :head], pairs[:, head:]
    for h in range(halves):
        if h > 0:
            relay(h)
        sums = []
        for c in range(2):
            p_copy(h, c, 0).wait_recv()
            p_copy(h, c, 2).wait_recv()
            sums.append(total[h, :, c * lane : (c + 1) * lane] + part_recv[h, c, 0] + part_recv[h, c, 2])
        full = jnp.concatenate(sums, axis=1)
        for n in range(half // head):
            queries = head_norm(full[:, n * head : (n + 1) * head], qg_ref[...]).astype(jnp.bfloat16)
            scores = lax.dot_general(
                queries, keys, (((1,), (1,)), ((), ())), preferred_element_type=jnp.float32
            ) * head ** (-0.5)
            scores = jnp.where(allowed, scores, masked_score)
            weights = jnp.exp(scores - jnp.max(scores, axis=1, keepdims=True)).astype(jnp.bfloat16)
            denominator = jnp.sum(weights.astype(jnp.float32), axis=1, keepdims=True)
            numerator = jnp.dot(weights, values, preferred_element_type=jnp.float32)
            place = h * half + n * head
            out_ref[:, place : place + head] = (numerator / denominator * factor).astype(jnp.bfloat16)

    for h in range(halves):
        for step in range(line - 1):
            for way in range(2):
                @pl.when(w_sends(step, way))
                def _():
                    w_copy(h, step, way).wait_send()
        for c in range(2):
            for number in range(3):
                p_copy(h, c, number).wait_send()
    for d in range(1, group):
        for t in range(pieces):
            t_copy(d, t).wait_send()
            for j in range(1, images):
                f_copy(d, t, j).wait_send()
    for j in range(1, images):
        s_copy(j).wait_send()
    drain(vis_send.at[pl.ds(0, shards - 1)], v_send.at[0])
    drain(pair_send.at[pl.ds(0, line - 1)], v_send.at[1])
    drain(pair_near, v_send.at[2])
    drain(kv_all.at[pl.ds(0, group - 1)], v_send.at[3])
    drain(kv_all.at[pl.ds(0, shards - group)], v_send.at[4])


def on_device(
    text_states, text_gain, vision, q_weight, k_weight, v_weight, q_gain, k_gain, owners, counts, gate_value,
):
    images = lax.axis_size("img")
    shards = lax.axis_size("fsdp")
    group, halves, pieces = 4, 2, 2
    line = shards // group
    rows, width = text_states.shape
    depth, columns = q_weight.shape
    half = columns // halves
    tokens = vision.shape[1]
    head = q_gain.shape[0]
    bf16, f32 = jnp.bfloat16, jnp.float32
    vmem = pl.BlockSpec(memory_space=pltpu.VMEM)
    smem = pl.BlockSpec(memory_space=pltpu.SMEM)
    dma = pltpu.SemaphoreType.DMA
    return pl.pallas_call(
        functools.partial(kernel, images, shards, group, halves, pieces),
        out_shape=jax.ShapeDtypeStruct((rows, columns), bf16),
        in_specs=[pl.BlockSpec(memory_space=pl.ANY)] + [vmem] * 7 + [smem, smem, vmem],
        out_specs=vmem,
        scratch_shapes=[
            pltpu.VMEM((rows, width), bf16),
            pltpu.VMEM((group, rows, line * depth), bf16),
            pltpu.VMEM((group - 1, rows, line * depth), bf16),
            pltpu.VMEM((halves, line, depth, half), bf16),
            pltpu.VMEM((halves, rows, half), f32),
            pltpu.VMEM((halves, 2, group - 1, rows, half // 2), f32),
            pltpu.VMEM((halves, 2, group - 1, rows, half // 2), f32),
            pltpu.VMEM((shards, tokens, depth), f32),
            pltpu.VMEM((images, shards, tokens, depth), f32),
            pltpu.VMEM((line, group, images, tokens, 2 * head), f32),
            pltpu.VMEM((line, group, images, tokens, 2 * head), f32),
            pltpu.VMEM((group, images, tokens, 2 * head), f32),
            pltpu.VMEM((group - 1, images, tokens, 2 * head), f32),
            pltpu.VMEM((images * tokens, 2 * head), bf16),
            pltpu.VMEM((shards, images * tokens, 2 * head), bf16),
            dma((halves, line - 1, 2)),
            dma((halves, line - 1, 2)),
            dma((group - 1, pieces)),
            dma((group - 1, pieces)),
            dma((group - 1, pieces, images - 1)),
            dma((group - 1, pieces, images - 1)),
            dma((halves, 2, 3)),
            dma((halves, 2, 3)),
            dma((5,)),
            dma((5,)),
            dma((images - 1,)),
            dma((images - 1,)),
            dma((images,)),
        ],
        compiler_params=pltpu.CompilerParams(
            collective_id=0, has_side_effects=True, vmem_limit_bytes=56 * 2**20
        ),
    )(
        text_states, text_gain[None], vision, q_weight, k_weight, v_weight, q_gain[None], k_gain[None],
        owners, counts, gate_value[None],
    )


def solution(mesh):
    in_specs = (
        P("fsdp", None),
        P(),
        P("img", "fsdp", None),
        P("fsdp", "img"),
        P("fsdp", "img"),
        P("fsdp", "img"),
        P(),
        P(),
        P("fsdp", None),
        P("fsdp"),
        P(),
    )
    out_specs = P("fsdp", "img")
    return jax.shard_map(
        on_device, mesh=mesh, in_specs=in_specs, out_specs=out_specs, check_vma=False
    )
```

```python
import functools

import jax
import jax.numpy as jnp
from jax import lax
from jax.experimental import pallas as pl
from jax.experimental.pallas import tpu as pltpu
from jax.sharding import PartitionSpec as P

norm_epsilon = 1e-05
masked_score = -1e30
MESH = pl.DeviceIdType.MESH
row_tile = 16


def head_norm(values, gain):
    mean_square = jnp.mean(values * values, axis=-1, keepdims=True)
    return values * lax.rsqrt(mean_square + norm_epsilon) * gain


def kernel(
    images, shards, group, parts, pieces,
    text_hbm, gain_ref, vision_ref, q_ref, k_ref, v_ref, qg_ref, kg_ref, owners_ref, counts_ref, gate_ref,
    out_ref,
    text_ref, normed, others, wbuf, total, part_send, part_recv,
    vis_send, vis_all, pair_send, pair_recv, pair_plane, pair_near, kv_own, kv_all,
    w_send, w_recv, t_send, t_recv, f_send, f_recv, p_send, p_recv, v_send, v_recv, s_send, s_recv, load,
):
    img = lax.axis_index("img")
    me = lax.axis_index("fsdp")
    line = shards // group
    along = lax.div(me, group)
    member = lax.rem(me, group)
    rows, width = text_hbm.shape
    depth, columns = q_ref.shape
    half = columns // parts
    head = qg_ref.shape[1]
    tokens = vision_ref.shape[1]
    part_rows = rows // images
    piece_rows = part_rows // pieces

    def copy(src, dst, send, recv, target):
        return pltpu.make_async_remote_copy(
            src_ref=src, dst_ref=dst, send_sem=send, recv_sem=recv, device_id=target, device_id_type=MESH
        )

    def drain(ref, sem):
        pltpu.make_async_copy(ref, ref, sem).wait()

    barrier = pltpu.get_barrier_semaphore()

    def greet(step, carry):
        pl.semaphore_signal(barrier, inc=1, device_id={"fsdp": lax.rem(me + step, shards)}, device_id_type=MESH)
        return carry

    lax.fori_loop(1, shards, greet, 0)
    for j in range(1, images):
        pl.semaphore_signal(barrier, inc=1, device_id={"img": lax.rem(img + j, images)}, device_id_type=MESH)
    def t_load(j):
        span = pl.ds(pl.multiple_of(lax.rem(img + j, images) * part_rows, part_rows), part_rows)
        return pltpu.make_async_copy(text_hbm.at[span], text_ref.at[span], load.at[j])

    for j in range(images):
        t_load(j).start()
    for h in range(parts):
        wbuf[h, along] = q_ref[:, h * half : (h + 1) * half]
    for f in range(shards):
        vis_send[f] = vision_ref[0, :, f * depth : (f + 1) * depth].astype(jnp.float32)
    vis_all[img, me] = vis_send[me]
    pl.semaphore_wait(barrier, shards - 1 + images - 1)

    def w_copy(h, step, way):
        slot = along - step if way == 0 else along + step
        to = me + group if way == 0 else me - group
        return copy(
            wbuf.at[h, slot], wbuf.at[h, slot], w_send.at[h, step, way], w_recv.at[h, step, way], {"fsdp": to}
        )

    def w_sends(step, way):
        if way == 0:
            return (along - step >= 0) & (along + 1 < line)
        return (along + step < line) & (along >= 1)

    def w_gets(step, way):
        if way == 0:
            return along - 1 - step >= 0
        return along + 1 + step < line

    def w_start(h, step):
        for way in range(2):
            @pl.when(w_sends(step, way))
            def _():
                w_copy(h, step, way).start()

    def w_arrive(h, step):
        for way in range(2):
            @pl.when(w_gets(step, way))
            def _():
                w_copy(h, step, way).wait_recv()
        if step + 1 < line - 1:
            w_start(h, step + 1)
        if step == 0 and h + 2 < parts:
            w_start(h + 2, 0)

    def spread(source, target, send, recv):
        def one(step, carry):
            to = lax.rem(me + step, shards)
            copy(source(to), target, send, recv, {"fsdp": to}).start()
            return carry

        lax.fori_loop(1, shards, one, 0)

    w_start(0, 0)
    w_start(1, 0)
    spread(lambda to: vis_send.at[to], vis_all.at[img, me], v_send.at[0], v_recv.at[0])

    def scale_of(row):
        acc = jnp.zeros((row_tile, depth), jnp.float32)
        for f in range(shards):
            x = text_ref[pl.ds(row, row_tile), f * depth : (f + 1) * depth].astype(jnp.float32)
            acc = acc + x * x
        return lax.rsqrt(jnp.sum(acc, axis=1, keepdims=True) / width + norm_epsilon)

    def norm_all(t, carry):
        row = pl.multiple_of(img * part_rows + t * row_tile, row_tile)
        scale = scale_of(row)
        for f in range(shards):
            span = slice(f * depth, (f + 1) * depth)
            x = text_ref[pl.ds(row, row_tile), span].astype(jnp.float32)
            place = f // group * depth
            normed[f % group, pl.ds(row, row_tile), place : place + depth] = (x * scale * gain_ref[:, span]).astype(
                jnp.bfloat16
            )
        return carry

    def partner(d):
        low = lax.rem(lax.rem(member, 2) + d % 2, 2)
        high = lax.rem(lax.div(member, 2) + d // 2, 2)
        return high * 2 + low

    def piece(t):
        return pl.ds(pl.multiple_of(img * part_rows + t * piece_rows, piece_rows), piece_rows)

    def t_copy(d, t):
        to = partner(d)
        return copy(
            normed.at[to, piece(t)], others.at[d - 1, piece(t)], t_send.at[d - 1, t], t_recv.at[d - 1, t],
            {"fsdp": along * group + to},
        )

    t_load(0).wait()
    steps = piece_rows // row_tile
    for t in range(pieces):
        lax.fori_loop(t * steps, (t + 1) * steps, norm_all, 0)
        for d in (1, 2):
            t_copy(d, t).start()

    for t in range(pieces):
        t_copy(3, t).start()

    for j in range(1, images):
        t_load(j).wait()

        def norm_own(t, carry):
            row = pl.multiple_of(lax.rem(img + j, images) * part_rows + t * row_tile, row_tile)
            scale = scale_of(row)
            for a in range(line):
                span = pl.ds(pl.multiple_of((a * group + member) * depth, depth), depth)
                x = text_ref[pl.ds(row, row_tile), span].astype(jnp.float32)
                normed[member, pl.ds(row, row_tile), a * depth : (a + 1) * depth] = (
                    x * scale * gain_ref[:, span]
                ).astype(jnp.bfloat16)
            return carry

        lax.fori_loop(0, part_rows // row_tile, norm_own, 0)

    drain(vis_all.at[img, pl.ds(0, shards - 1)], v_recv.at[0])

    def s_copy(j):
        return copy(
            vis_all.at[img], vis_all.at[img], s_send.at[j - 1], s_recv.at[j - 1], {"img": lax.rem(img + j, images)}
        )

    for j in range(1, images):
        s_copy(j).start()
    w_arrive(0, 0)
    for j in range(1, images):
        s_copy(j).wait_recv()
    for m in range(images):
        x = vis_all[m].reshape(shards * tokens, depth).astype(jnp.bfloat16)
        keys_part = jnp.dot(x, k_ref[...], preferred_element_type=jnp.float32)
        values_part = jnp.dot(x, v_ref[...], preferred_element_type=jnp.float32)
        pair_send[:, :, m, :, :head] = keys_part.reshape(line, group, tokens, head)
        pair_send[:, :, m, :, head:] = values_part.reshape(line, group, tokens, head)

    def along_line(source, target, number):
        def one(step, carry):
            to = lax.rem(along + step, line)
            copy(source(to), target, v_send.at[number], v_recv.at[number], {"fsdp": to * group + member}).start()
            return carry

        lax.fori_loop(1, line, one, 0)

    def over_plane(source, target, number):
        for d in range(1, group):
            to = partner(d)
            copy(
                source(to), target(d), v_send.at[number], v_recv.at[number], {"fsdp": along * group + to}
            ).start()

    along_line(lambda to: pair_send.at[to], pair_recv.at[along], 1)
    pair_recv[along] = pair_send[along]
    for step in range(1, line - 1):
        w_arrive(0, step)
    for step in range(line - 1):
        w_arrive(1, step)
    drain(pair_recv.at[pl.ds(0, line - 1)], v_recv.at[1])
    pair_plane[...] = jnp.sum(pair_recv[...], axis=0)
    over_plane(lambda to: pair_plane.at[to], lambda d: pair_near.at[d - 1], 2)

    def f_copy(d, t, j):
        return copy(
            others.at[d - 1, piece(t)], others.at[d - 1, piece(t)],
            f_send.at[d - 1, t, j - 1], f_recv.at[d - 1, t, j - 1], {"img": lax.rem(img + j, images)},
        )

    def t_arrive(d):
        for t in range(pieces):
            t_copy(d, t).wait_recv()
            for j in range(1, images):
                f_copy(d, t, j).start()

    def f_arrive(d):
        for t in range(pieces):
            for j in range(1, images):
                f_copy(d, t, j).wait_recv()

    def p_copy(h, c, number):
        first, second = (1, 2) if c == 0 else (2, 1)
        source = (first, 3, second)[number] - 1
        over = second if number == 2 else first
        return copy(
            part_send.at[h, c, source], part_recv.at[h, c, number], p_send.at[h, c, number],
            p_recv.at[h, c, number], {"fsdp": along * group + partner(over)},
        )

    lane = rows // 2

    def project(h, d):
        weight = wbuf[h].reshape(line * depth, half)
        product = jnp.dot(
            normed[member] if d == 0 else others[d - 1], weight, preferred_element_type=jnp.float32
        )
        if d == 0:
            total[h] = product
            return
        for c in range(2):
            part_send[h, c, d - 1] = product[c * lane : (c + 1) * lane]
        if d == 3:
            p_copy(h, 0, 1).start()
            p_copy(h, 1, 1).start()
        else:
            p_copy(h, d - 1, 0).start()

    def relay(h):
        for c in range(2):
            p_copy(h, c, 1).wait_recv()
            second = 2 if c == 0 else 1
            part_send[h, c, second - 1] = part_send[h, c, second - 1] + part_recv[h, c, 1]
            p_copy(h, c, 2).start()

    t_arrive(1)
    t_arrive(2)
    w_arrive(2, 0)
    f_arrive(1)
    project(0, 1)
    f_arrive(2)
    project(0, 2)
    w_arrive(2, 1)
    t_arrive(3)
    f_arrive(3)
    project(0, 3)
    for step in range(2, line - 1):
        w_arrive(2, step)
    project(0, 0)
    for d in (3, 1, 2):
        project(1, d)
    w_arrive(3, 0)
    drain(pair_near, v_recv.at[2])
    pair = pair_plane[member]
    for d in range(1, group):
        pair = pair + pair_near[d - 1]
    pair = pair.reshape(images * tokens, 2 * head)
    kv_own[:, :head] = head_norm(pair[:, :head], kg_ref[...]).astype(jnp.bfloat16)
    kv_own[:, head:] = pair[:, head:].astype(jnp.bfloat16)
    over_plane(lambda to: kv_own, lambda d: kv_all.at[me], 3)
    kv_all[me] = kv_own[...]
    project(1, 0)
    relay(0)
    w_arrive(3, 1)
    for d in (3, 1, 2, 0):
        project(2, d)
    relay(1)
    drain(kv_all.at[pl.ds(0, group - 1)], v_recv.at[3])
    plane = pl.ds(along * group, group)
    along_line(lambda to: kv_all.at[plane], kv_all.at[plane], 4)
    for step in range(2, line - 1):
        w_arrive(3, step)
    for d in (3, 1, 2, 0):
        project(3, d)
    relay(2)

    drain(kv_all.at[pl.ds(0, shards - group)], v_recv.at[4])
    key_count = shards * images * tokens
    blocks = owners_ref.shape[0]
    key_image = lax.rem(lax.div(lax.broadcasted_iota(jnp.int32, (1, key_count), 1), tokens), images)
    gate = jnp.tanh(gate_ref[...])
    masks, factors = [], []
    for blk in range(blocks):
        row = jnp.zeros((1, key_count), jnp.int32)
        live = jnp.int32(0)
        for m in range(images):
            hit = jnp.int32(0)
            for slot in range(owners_ref.shape[1]):
                same = jnp.where(owners_ref[blk, slot] == m, 1, 0)
                hit = jnp.maximum(hit, jnp.where(slot < counts_ref[blk], same, 0))
            row = jnp.where(key_image == m, hit, row)
            live = jnp.maximum(live, hit)
        masks.append(jnp.broadcast_to(row, (rows // blocks, key_count)))
        factors.append(jnp.broadcast_to(gate * live.astype(jnp.float32), (rows // blocks, 1)))
    allowed = jnp.concatenate(masks, axis=0) > 0
    factor = jnp.concatenate(factors, axis=0)
    pairs = kv_all[...].reshape(key_count, 2 * head)
    keys, values = pairs[:, :head], pairs[:, head:]
    for h in range(parts):
        if h == parts - 2:
            relay(h + 1)
        sums = []
        for c in range(2):
            p_copy(h, c, 0).wait_recv()
            p_copy(h, c, 2).wait_recv()
            sums.append(total[h, c * lane : (c + 1) * lane] + part_recv[h, c, 0] + part_recv[h, c, 2])
        full = jnp.concatenate(sums, axis=0)
        for n in range(half // head):
            queries = head_norm(full[:, n * head : (n + 1) * head], qg_ref[...]).astype(jnp.bfloat16)
            scores = lax.dot_general(
                queries, keys, (((1,), (1,)), ((), ())), preferred_element_type=jnp.float32
            ) * head ** (-0.5)
            scores = jnp.where(allowed, scores, masked_score)
            weights = jnp.exp(scores - jnp.max(scores, axis=1, keepdims=True)).astype(jnp.bfloat16)
            denominator = jnp.sum(weights.astype(jnp.float32), axis=1, keepdims=True)
            numerator = jnp.dot(weights, values, preferred_element_type=jnp.float32)
            place = h * half + n * head
            out_ref[:, place : place + head] = (numerator / denominator * factor).astype(jnp.bfloat16)

    for h in range(parts):
        for step in range(line - 1):
            for way in range(2):
                @pl.when(w_sends(step, way))
                def _():
                    w_copy(h, step, way).wait_send()
        for c in range(2):
            for number in range(3):
                p_copy(h, c, number).wait_send()
    for d in range(1, group):
        for t in range(pieces):
            t_copy(d, t).wait_send()
            for j in range(1, images):
                f_copy(d, t, j).wait_send()
    for j in range(1, images):
        s_copy(j).wait_send()
    drain(vis_send.at[pl.ds(0, shards - 1)], v_send.at[0])
    drain(pair_send.at[pl.ds(0, line - 1)], v_send.at[1])
    drain(pair_near, v_send.at[2])
    drain(kv_all.at[pl.ds(0, group - 1)], v_send.at[3])
    drain(kv_all.at[pl.ds(0, shards - group)], v_send.at[4])


def on_device(
    text_states, text_gain, vision, q_weight, k_weight, v_weight, q_gain, k_gain, owners, counts, gate_value,
):
    images = lax.axis_size("img")
    shards = lax.axis_size("fsdp")
    group, parts, pieces = 4, 4, 2
    line = shards // group
    rows, width = text_states.shape
    depth, columns = q_weight.shape
    half = columns // parts
    tokens = vision.shape[1]
    head = q_gain.shape[0]
    bf16, f32 = jnp.bfloat16, jnp.float32
    vmem = pl.BlockSpec(memory_space=pltpu.VMEM)
    smem = pl.BlockSpec(memory_space=pltpu.SMEM)
    dma = pltpu.SemaphoreType.DMA
    return pl.pallas_call(
        functools.partial(kernel, images, shards, group, parts, pieces),
        out_shape=jax.ShapeDtypeStruct((rows, columns), bf16),
        in_specs=[pl.BlockSpec(memory_space=pl.ANY)] + [vmem] * 7 + [smem, smem, vmem],
        out_specs=vmem,
        scratch_shapes=[
            pltpu.VMEM((rows, width), bf16),
            pltpu.VMEM((group, rows, line * depth), bf16),
            pltpu.VMEM((group - 1, rows, line * depth), bf16),
            pltpu.VMEM((parts, line, depth, half), bf16),
            pltpu.VMEM((parts, rows, half), f32),
            pltpu.VMEM((parts, 2, group - 1, rows // 2, half), f32),
            pltpu.VMEM((parts, 2, group - 1, rows // 2, half), f32),
            pltpu.VMEM((shards, tokens, depth), f32),
            pltpu.VMEM((images, shards, tokens, depth), f32),
            pltpu.VMEM((line, group, images, tokens, 2 * head), f32),
            pltpu.VMEM((line, group, images, tokens, 2 * head), f32),
            pltpu.VMEM((group, images, tokens, 2 * head), f32),
            pltpu.VMEM((group - 1, images, tokens, 2 * head), f32),
            pltpu.VMEM((images * tokens, 2 * head), bf16),
            pltpu.VMEM((shards, images * tokens, 2 * head), bf16),
            dma((parts, line - 1, 2)),
            dma((parts, line - 1, 2)),
            dma((group - 1, pieces)),
            dma((group - 1, pieces)),
            dma((group - 1, pieces, images - 1)),
            dma((group - 1, pieces, images - 1)),
            dma((parts, 2, 3)),
            dma((parts, 2, 3)),
            dma((5,)),
            dma((5,)),
            dma((images - 1,)),
            dma((images - 1,)),
            dma((images,)),
        ],
        compiler_params=pltpu.CompilerParams(
            collective_id=0, has_side_effects=True, vmem_limit_bytes=56 * 2**20
        ),
    )(
        text_states, text_gain[None], vision, q_weight, k_weight, v_weight, q_gain[None], k_gain[None],
        owners, counts, gate_value[None],
    )


def solution(mesh):
    in_specs = (
        P("fsdp", None),
        P(),
        P("img", "fsdp", None),
        P("fsdp", "img"),
        P("fsdp", "img"),
        P("fsdp", "img"),
        P(),
        P(),
        P("fsdp", None),
        P("fsdp"),
        P(),
    )
    out_specs = P("fsdp", "img")
    return jax.shard_map(
        on_device, mesh=mesh, in_specs=in_specs, out_specs=out_specs, check_vma=False
    )
```

```python
import functools

import jax
import jax.numpy as jnp
from jax import lax
from jax.experimental import pallas as pl
from jax.experimental.pallas import tpu as pltpu
from jax.sharding import PartitionSpec as P

norm_epsilon = 1e-05
masked_score = -1e30
MESH = pl.DeviceIdType.MESH
row_tile = 16


def head_norm(values, gain):
    mean_square = jnp.mean(values * values, axis=-1, keepdims=True)
    return values * lax.rsqrt(mean_square + norm_epsilon) * gain


def kernel(
    images, shards, group, parts, pieces,
    text_hbm, gain_ref, vision_ref, q_ref, k_ref, v_ref, qg_ref, kg_ref, owners_ref, counts_ref, gate_ref,
    out_ref,
    text_ref, normed, others, wbuf, total, part_send, part_recv,
    vis_send, vis_all, pair_send, pair_recv, pair_plane, pair_near, kv_own, kv_all,
    w_send, w_recv, t_send, t_recv, f_send, f_recv, p_send, p_recv, v_send, v_recv, s_send, s_recv, load, hop, h_send, h_recv,
):
    img = lax.axis_index("img")
    me = lax.axis_index("fsdp")
    line = shards // group
    along = lax.div(me, group)
    member = lax.rem(me, group)
    rows, width = text_hbm.shape
    depth, columns = q_ref.shape
    half = columns // parts
    head = qg_ref.shape[1]
    tokens = vision_ref.shape[1]
    part_rows = rows // images
    piece_rows = part_rows // pieces

    def copy(src, dst, send, recv, target):
        return pltpu.make_async_remote_copy(
            src_ref=src, dst_ref=dst, send_sem=send, recv_sem=recv, device_id=target, device_id_type=MESH
        )

    def drain(ref, sem):
        pltpu.make_async_copy(ref, ref, sem).wait()

    barrier = pltpu.get_barrier_semaphore()

    def greet(step, carry):
        pl.semaphore_signal(barrier, inc=1, device_id={"fsdp": lax.rem(me + step, shards)}, device_id_type=MESH)
        return carry

    lax.fori_loop(1, shards, greet, 0)
    for j in range(1, images):
        pl.semaphore_signal(barrier, inc=1, device_id={"img": lax.rem(img + j, images)}, device_id_type=MESH)
    def t_load(j):
        span = pl.ds(pl.multiple_of(lax.rem(img + j, images) * part_rows, part_rows), part_rows)
        return pltpu.make_async_copy(text_hbm.at[span], text_ref.at[span], load.at[j])

    for j in range(images):
        t_load(j).start()
    for h in range(parts):
        wbuf[h, along] = q_ref[:, h * half : (h + 1) * half]
    for f in range(shards):
        vis_send[f] = vision_ref[0, :, f * depth : (f + 1) * depth].astype(jnp.float32)
    vis_all[img, me] = vis_send[me]
    pl.semaphore_wait(barrier, shards - 1 + images - 1)

    def w_copy(h, step, way):
        slot = along - step if way == 0 else along + step
        to = me + group if way == 0 else me - group
        return copy(
            wbuf.at[h, slot], wbuf.at[h, slot], w_send.at[h, step, way], w_recv.at[h, step, way], {"fsdp": to}
        )

    def w_sends(step, way):
        if way == 0:
            return (along - step >= 0) & (along + 1 < line)
        return (along + step < line) & (along >= 1)

    def w_gets(step, way):
        if way == 0:
            return along - 1 - step >= 0
        return along + 1 + step < line

    def w_start(h, step):
        for way in range(2):
            @pl.when(w_sends(step, way))
            def _():
                w_copy(h, step, way).start()

    def w_arrive(h, step):
        for way in range(2):
            @pl.when(w_gets(step, way))
            def _():
                w_copy(h, step, way).wait_recv()
        if step + 1 < line - 1:
            w_start(h, step + 1)
        if step == 0 and h + 2 < parts:
            w_start(h + 2, 0)

    def spread(source, target, send, recv):
        def one(step, carry):
            to = lax.rem(me + step, shards)
            copy(source(to), target, send, recv, {"fsdp": to}).start()
            return carry

        lax.fori_loop(1, shards, one, 0)

    w_start(0, 0)
    w_start(1, 0)
    spread(lambda to: vis_send.at[to], vis_all.at[img, me], v_send.at[0], v_recv.at[0])

    def scale_of(row):
        acc = jnp.zeros((row_tile, depth), jnp.float32)
        for f in range(shards):
            x = text_ref[pl.ds(row, row_tile), f * depth : (f + 1) * depth].astype(jnp.float32)
            acc = acc + x * x
        return lax.rsqrt(jnp.sum(acc, axis=1, keepdims=True) / width + norm_epsilon)

    def norm_all(t, carry):
        row = pl.multiple_of(img * part_rows + t * row_tile, row_tile)
        scale = scale_of(row)
        for f in range(shards):
            span = slice(f * depth, (f + 1) * depth)
            x = text_ref[pl.ds(row, row_tile), span].astype(jnp.float32)
            place = f // group * depth
            normed[f % group, pl.ds(row, row_tile), place : place + depth] = (x * scale * gain_ref[:, span]).astype(
                jnp.bfloat16
            )
        return carry

    def partner(d):
        low = lax.rem(lax.rem(member, 2) + d % 2, 2)
        high = lax.rem(lax.div(member, 2) + d // 2, 2)
        return high * 2 + low

    def piece(t):
        return pl.ds(pl.multiple_of(img * part_rows + t * piece_rows, piece_rows), piece_rows)

    def t_copy(d, t):
        to = partner(d if d < 3 else 2 - t)
        source = normed.at[to, piece(t)] if d < 3 else hop.at[t]
        return copy(
            source, others.at[d - 1, piece(t)], t_send.at[d - 1, t], t_recv.at[d - 1, t],
            {"fsdp": along * group + to},
        )

    def h_copy(t):
        return copy(
            normed.at[partner(3), piece(t)], hop.at[t], h_send.at[t], h_recv.at[t],
            {"fsdp": along * group + partner(t + 1)},
        )

    t_load(0).wait()
    steps = piece_rows // row_tile
    for t in range(pieces):
        lax.fori_loop(t * steps, (t + 1) * steps, norm_all, 0)
        for d in (1, 2):
            t_copy(d, t).start()

    for t in range(pieces):
        h_copy(t).start()

    for j in range(1, images):
        t_load(j).wait()

        def norm_own(t, carry):
            row = pl.multiple_of(lax.rem(img + j, images) * part_rows + t * row_tile, row_tile)
            scale = scale_of(row)
            for a in range(line):
                span = pl.ds(pl.multiple_of((a * group + member) * depth, depth), depth)
                x = text_ref[pl.ds(row, row_tile), span].astype(jnp.float32)
                normed[member, pl.ds(row, row_tile), a * depth : (a + 1) * depth] = (
                    x * scale * gain_ref[:, span]
                ).astype(jnp.bfloat16)
            return carry

        lax.fori_loop(0, part_rows // row_tile, norm_own, 0)

    drain(vis_all.at[img, pl.ds(0, shards - 1)], v_recv.at[0])

    def s_copy(j):
        return copy(
            vis_all.at[img], vis_all.at[img], s_send.at[j - 1], s_recv.at[j - 1], {"img": lax.rem(img + j, images)}
        )

    for j in range(1, images):
        s_copy(j).start()
    w_arrive(0, 0)
    for j in range(1, images):
        s_copy(j).wait_recv()
    for m in range(images):
        x = vis_all[m].reshape(shards * tokens, depth).astype(jnp.bfloat16)
        keys_part = jnp.dot(x, k_ref[...], preferred_element_type=jnp.float32)
        values_part = jnp.dot(x, v_ref[...], preferred_element_type=jnp.float32)
        pair_send[:, :, m, :, :head] = keys_part.reshape(line, group, tokens, head)
        pair_send[:, :, m, :, head:] = values_part.reshape(line, group, tokens, head)

    def along_line(source, target, number):
        def one(step, carry):
            to = lax.rem(along + step, line)
            copy(source(to), target, v_send.at[number], v_recv.at[number], {"fsdp": to * group + member}).start()
            return carry

        lax.fori_loop(1, line, one, 0)

    def over_plane(source, target, number):
        for d in range(1, group):
            to = partner(d)
            copy(
                source(to), target(d), v_send.at[number], v_recv.at[number], {"fsdp": along * group + to}
            ).start()

    along_line(lambda to: pair_send.at[to], pair_recv.at[along], 1)
    pair_recv[along] = pair_send[along]
    for step in range(1, line - 1):
        w_arrive(0, step)
    for step in range(line - 1):
        w_arrive(1, step)
    drain(pair_recv.at[pl.ds(0, line - 1)], v_recv.at[1])
    pair_plane[...] = jnp.sum(pair_recv[...], axis=0)
    over_plane(lambda to: pair_plane.at[to], lambda d: pair_near.at[d - 1], 2)

    def f_copy(d, t, j):
        return copy(
            others.at[d - 1, piece(t)], others.at[d - 1, piece(t)],
            f_send.at[d - 1, t, j - 1], f_recv.at[d - 1, t, j - 1], {"img": lax.rem(img + j, images)},
        )

    def t_arrive(d):
        for t in range(pieces):
            t_copy(d, t).wait_recv()
            for j in range(1, images):
                f_copy(d, t, j).start()

    def f_arrive(d):
        for t in range(pieces):
            for j in range(1, images):
                f_copy(d, t, j).wait_recv()

    def p_copy(h, c, number):
        first, second = (1, 2) if c == 0 else (2, 1)
        source = (first, 3, second)[number] - 1
        over = second if number == 2 else first
        return copy(
            part_send.at[h, c, source], part_recv.at[h, c, number], p_send.at[h, c, number],
            p_recv.at[h, c, number], {"fsdp": along * group + partner(over)},
        )

    lane = rows // 2

    def project(h, d):
        weight = wbuf[h].reshape(line * depth, half)
        product = jnp.dot(
            normed[member] if d == 0 else others[d - 1], weight, preferred_element_type=jnp.float32
        )
        if d == 0:
            total[h] = product
            return
        for c in range(2):
            part_send[h, c, d - 1] = product[c * lane : (c + 1) * lane]
        if d == 3:
            p_copy(h, 0, 1).start()
            p_copy(h, 1, 1).start()
        else:
            p_copy(h, d - 1, 0).start()

    def relay(h):
        for c in range(2):
            p_copy(h, c, 1).wait_recv()
            second = 2 if c == 0 else 1
            part_send[h, c, second - 1] = part_send[h, c, second - 1] + part_recv[h, c, 1]
            p_copy(h, c, 2).start()

    t_arrive(1)
    t_arrive(2)
    for t in range(pieces):
        h_copy(t).wait_recv()
        t_copy(3, t).start()
    w_arrive(2, 0)
    f_arrive(1)
    project(0, 1)
    f_arrive(2)
    project(0, 2)
    w_arrive(2, 1)
    t_arrive(3)
    f_arrive(3)
    project(0, 3)
    for step in range(2, line - 1):
        w_arrive(2, step)
    project(0, 0)
    for d in (3, 1, 2):
        project(1, d)
    w_arrive(3, 0)
    drain(pair_near, v_recv.at[2])
    pair = pair_plane[member]
    for d in range(1, group):
        pair = pair + pair_near[d - 1]
    pair = pair.reshape(images * tokens, 2 * head)
    kv_own[:, :head] = head_norm(pair[:, :head], kg_ref[...]).astype(jnp.bfloat16)
    kv_own[:, head:] = pair[:, head:].astype(jnp.bfloat16)
    over_plane(lambda to: kv_own, lambda d: kv_all.at[me], 3)
    kv_all[me] = kv_own[...]
    project(1, 0)
    relay(0)
    w_arrive(3, 1)
    for d in (3, 1, 2, 0):
        project(2, d)
    relay(1)
    drain(kv_all.at[pl.ds(0, group - 1)], v_recv.at[3])
    plane = pl.ds(along * group, group)
    along_line(lambda to: kv_all.at[plane], kv_all.at[plane], 4)
    for step in range(2, line - 1):
        w_arrive(3, step)
    for d in (3, 1, 2, 0):
        project(3, d)
    relay(2)

    drain(kv_all.at[pl.ds(0, shards - group)], v_recv.at[4])
    key_count = shards * images * tokens
    blocks = owners_ref.shape[0]
    key_image = lax.rem(lax.div(lax.broadcasted_iota(jnp.int32, (1, key_count), 1), tokens), images)
    gate = jnp.tanh(gate_ref[...])
    masks, factors = [], []
    for blk in range(blocks):
        row = jnp.zeros((1, key_count), jnp.int32)
        live = jnp.int32(0)
        for m in range(images):
            hit = jnp.int32(0)
            for slot in range(owners_ref.shape[1]):
                same = jnp.where(owners_ref[blk, slot] == m, 1, 0)
                hit = jnp.maximum(hit, jnp.where(slot < counts_ref[blk], same, 0))
            row = jnp.where(key_image == m, hit, row)
            live = jnp.maximum(live, hit)
        masks.append(jnp.broadcast_to(row, (rows // blocks, key_count)))
        factors.append(jnp.broadcast_to(gate * live.astype(jnp.float32), (rows // blocks, 1)))
    allowed = jnp.concatenate(masks, axis=0) > 0
    factor = jnp.concatenate(factors, axis=0)
    pairs = kv_all[...].reshape(key_count, 2 * head)
    keys, values = pairs[:, :head], pairs[:, head:]
    for h in range(parts):
        if h == parts - 2:
            relay(h + 1)
        sums = []
        for c in range(2):
            p_copy(h, c, 0).wait_recv()
            p_copy(h, c, 2).wait_recv()
            sums.append(total[h, c * lane : (c + 1) * lane] + part_recv[h, c, 0] + part_recv[h, c, 2])
        full = jnp.concatenate(sums, axis=0)
        for n in range(half // head):
            queries = head_norm(full[:, n * head : (n + 1) * head], qg_ref[...]).astype(jnp.bfloat16)
            scores = lax.dot_general(
                queries, keys, (((1,), (1,)), ((), ())), preferred_element_type=jnp.float32
            ) * head ** (-0.5)
            scores = jnp.where(allowed, scores, masked_score)
            weights = jnp.exp(scores - jnp.max(scores, axis=1, keepdims=True)).astype(jnp.bfloat16)
            denominator = jnp.sum(weights.astype(jnp.float32), axis=1, keepdims=True)
            numerator = jnp.dot(weights, values, preferred_element_type=jnp.float32)
            place = h * half + n * head
            out_ref[:, place : place + head] = (numerator / denominator * factor).astype(jnp.bfloat16)

    for h in range(parts):
        for step in range(line - 1):
            for way in range(2):
                @pl.when(w_sends(step, way))
                def _():
                    w_copy(h, step, way).wait_send()
        for c in range(2):
            for number in range(3):
                p_copy(h, c, number).wait_send()
    for d in range(1, group):
        for t in range(pieces):
            t_copy(d, t).wait_send()
            for j in range(1, images):
                f_copy(d, t, j).wait_send()
    for t in range(pieces):
        h_copy(t).wait_send()
    for j in range(1, images):
        s_copy(j).wait_send()
    drain(vis_send.at[pl.ds(0, shards - 1)], v_send.at[0])
    drain(pair_send.at[pl.ds(0, line - 1)], v_send.at[1])
    drain(pair_near, v_send.at[2])
    drain(kv_all.at[pl.ds(0, group - 1)], v_send.at[3])
    drain(kv_all.at[pl.ds(0, shards - group)], v_send.at[4])


def on_device(
    text_states, text_gain, vision, q_weight, k_weight, v_weight, q_gain, k_gain, owners, counts, gate_value,
):
    images = lax.axis_size("img")
    shards = lax.axis_size("fsdp")
    group, parts, pieces = 4, 4, 2
    line = shards // group
    rows, width = text_states.shape
    depth, columns = q_weight.shape
    half = columns // parts
    tokens = vision.shape[1]
    head = q_gain.shape[0]
    bf16, f32 = jnp.bfloat16, jnp.float32
    vmem = pl.BlockSpec(memory_space=pltpu.VMEM)
    smem = pl.BlockSpec(memory_space=pltpu.SMEM)
    dma = pltpu.SemaphoreType.DMA
    return pl.pallas_call(
        functools.partial(kernel, images, shards, group, parts, pieces),
        out_shape=jax.ShapeDtypeStruct((rows, columns), bf16),
        in_specs=[pl.BlockSpec(memory_space=pl.ANY)] + [vmem] * 7 + [smem, smem, vmem],
        out_specs=vmem,
        scratch_shapes=[
            pltpu.VMEM((rows, width), bf16),
            pltpu.VMEM((group, rows, line * depth), bf16),
            pltpu.VMEM((group - 1, rows, line * depth), bf16),
            pltpu.VMEM((parts, line, depth, half), bf16),
            pltpu.VMEM((parts, rows, half), f32),
            pltpu.VMEM((parts, 2, group - 1, rows // 2, half), f32),
            pltpu.VMEM((parts, 2, group - 1, rows // 2, half), f32),
            pltpu.VMEM((shards, tokens, depth), f32),
            pltpu.VMEM((images, shards, tokens, depth), f32),
            pltpu.VMEM((line, group, images, tokens, 2 * head), f32),
            pltpu.VMEM((line, group, images, tokens, 2 * head), f32),
            pltpu.VMEM((group, images, tokens, 2 * head), f32),
            pltpu.VMEM((group - 1, images, tokens, 2 * head), f32),
            pltpu.VMEM((images * tokens, 2 * head), bf16),
            pltpu.VMEM((shards, images * tokens, 2 * head), bf16),
            dma((parts, line - 1, 2)),
            dma((parts, line - 1, 2)),
            dma((group - 1, pieces)),
            dma((group - 1, pieces)),
            dma((group - 1, pieces, images - 1)),
            dma((group - 1, pieces, images - 1)),
            dma((parts, 2, 3)),
            dma((parts, 2, 3)),
            dma((5,)),
            dma((5,)),
            dma((images - 1,)),
            dma((images - 1,)),
            dma((images,)),
            pltpu.VMEM((pieces, rows // images // pieces, line * depth), bf16),
            dma((pieces,)),
            dma((pieces,)),
        ],
        compiler_params=pltpu.CompilerParams(
            collective_id=0, has_side_effects=True, vmem_limit_bytes=56 * 2**20
        ),
    )(
        text_states, text_gain[None], vision, q_weight, k_weight, v_weight, q_gain[None], k_gain[None],
        owners, counts, gate_value[None],
    )


def solution(mesh):
    in_specs = (
        P("fsdp", None),
        P(),
        P("img", "fsdp", None),
        P("fsdp", "img"),
        P("fsdp", "img"),
        P("fsdp", "img"),
        P(),
        P(),
        P("fsdp", None),
        P("fsdp"),
        P(),
    )
    out_specs = P("fsdp", "img")
    return jax.shard_map(
        on_device, mesh=mesh, in_specs=in_specs, out_specs=out_specs, check_vma=False
    )
```
